32 devices in a mesh: section: 2 (over core), dp: 8 (over z, x), mp: 2 (over y).
Axes of the slice: x: 2, y: 2, z: 4, core: 2. Of those that a mesh axis runs over, the one named last changes fastest.
Arguments:
- section_weights: bfloat16 [2, 12288, 12288], P('section', 'mp', 'dp'), may hold values from -0.0546875 to 0.0546875
- tensor_inputs: bfloat16 [2, 1024, 12288], P('section', 'dp', 'mp'), may hold values from -6 to 6
- stream_inputs: bfloat16 [2, 1024, 12288], P('section', 'mp', 'dp'), may hold values from -26 to 26
- ln_gain: float32 [12288], P('dp'), may hold values from 0.5 to 1.5
- ln_bias: float32 [12288], P('dp'), may hold values from -3 to 3
Outputs:
- handed_over: bfloat16 [2, 1024, 12288], P('section', 'mp', 'dp')
- section_outputs: bfloat16 [2, 1024, 12288], P('section', 'dp', 'mp')
The draws below stay inside these ranges and needn't reach their ends.
All inputs are finite; a program needn't handle non-finite values.
Results may differ from the reference program's by a relative error of at most 0.0056.
Values may be sent and summed in bfloat16 or wider, within the bound.
A program may use at most 128 MiB of HBM per device.

```python
import math
import jax
import jax.numpy as jnp
from jax import lax

D = 12288
TOKENS = 1024


def draw_stream_inputs(key, part):
    key = jax.random.fold_in(key, 11)
    key_base = jax.random.fold_in(key, 1)
    key_cols = jax.random.fold_in(key, 2)
    key_offset = jax.random.fold_in(key, 3)
    ramp = 3.0 ** (jnp.arange(D, dtype=jnp.float32) / D) / math.sqrt(3.0)
    column_scale = jnp.exp(jax.random.uniform(key_cols, (2, 1, D), jnp.float32, math.log(0.4), math.log(2.5))) * ramp
    offset = jax.random.uniform(key_offset, (2, TOKENS, 1), jnp.float32, -1.5, 1.5)
    base = jax.random.truncated_normal(key_base, -4.0, 4.0, (2, TOKENS, D), jnp.float32)
    values = base * column_scale + offset
    return values.astype(jnp.bfloat16)


def shard_levels(stream_key, dims, cuts, low, high):
    def one(dim, shards_of):
        heights = jax.random.uniform(jax.random.fold_in(jax.random.fold_in(stream_key, 6), dim), (shards_of,), jnp.float32, low / len(cuts), high / len(cuts))
        return jnp.repeat(jnp.exp(heights), dims[dim] // shards_of).reshape((-1,) + (1,) * (len(dims) - dim - 1))

    level = one(*cuts[0])
    for cut in cuts[1:]:
        level = level * one(*cut)
    return level


def centred(rng, dims, deviation, reach, cuts=(), held_as=jnp.bfloat16):
    level = shard_levels(rng, dims, cuts, -0.22, 0.18) if cuts else 1.0
    result = jax.random.normal(rng, dims, jnp.float32) * deviation * level
    return jnp.minimum(jnp.maximum(result, -reach), reach).astype(held_as)


def setup_inputs(seed: int = 0) -> dict:
    seeds = jax.random.split(jax.random.key(seed), 6)
    section_weights = centred(seeds[0], (2, D, D), D ** -0.5, 0.0546875, ((0, 2), (1, 2), (2, 8)))
    tensor_inputs = centred(seeds[1], (2, TOKENS, D), 1.0, 6.0, ((0, 2), (1, 8), (2, 2)))
    stream_inputs = draw_stream_inputs(jax.random.fold_in(seeds[5], 71), 0)
    ln_gain = jnp.clip(0.5 + 1.0 * jax.random.uniform(seeds[3], (D,), jnp.float32) ** shard_levels(seeds[3], (D,), ((0, 8),), -0.2, 0.2), 0.5, 1.5)
    ln_bias = centred(seeds[4], (D,), 0.5, 3.0, ((0, 8),), jnp.float32)
    return dict(section_weights=section_weights, tensor_inputs=tensor_inputs, stream_inputs=stream_inputs, ln_gain=ln_gain, ln_bias=ln_bias)


def moments(values):
    center = lax.optimization_barrier(jnp.mean(values, axis=-1, keepdims=True))
    spread = lax.optimization_barrier(jnp.mean(jnp.square(values - center), axis=-1, keepdims=True))
    return (center, lax.rsqrt(spread + 1e-05))

def transposed(left, right):
    return lax.dot_general(left, right, (((1,), (1,)), ((), ())), preferred_element_type=jnp.float32)

def reference(section_weights, tensor_inputs, stream_inputs, ln_gain, ln_bias):
    w_output = section_weights[0]
    w_query = section_weights[1]
    context = tensor_inputs[0]
    upstream = tensor_inputs[1]
    residual = stream_inputs[0]
    earlier = stream_inputs[1]
    boundary = (residual.astype(jnp.float32) + jnp.dot(context, w_output, preferred_element_type=jnp.float32)).astype(jnp.bfloat16)
    saved = earlier.astype(jnp.float32)
    center, inverse = moments(saved)
    normed = (saved - center) * inverse
    scaled = jnp.dot(upstream, w_query, preferred_element_type=jnp.float32) * ln_gain
    first_mean = lax.optimization_barrier(jnp.mean(scaled, axis=-1, keepdims=True))
    second_mean = lax.optimization_barrier(jnp.mean(scaled * normed, axis=-1, keepdims=True))
    returned = (inverse * (scaled - first_mean - normed * second_mean)).astype(jnp.bfloat16)
    context_grad = transposed(returned, w_output).astype(jnp.bfloat16)
    arrived = boundary.astype(jnp.float32)
    center_b, inverse_b = moments(arrived)
    normed_in = ((arrived - center_b) * inverse_b * ln_gain + ln_bias).astype(jnp.bfloat16)
    queries = transposed(normed_in, w_query).astype(jnp.bfloat16)
    return (jnp.stack([returned, boundary]), jnp.stack([context_grad, queries]))
```

```python
import functools

import jax
import jax.numpy as jnp
from jax import lax
from jax.experimental import pallas as pl
from jax.experimental.pallas import tpu as pltpu
from jax.sharding import PartitionSpec as P

D = 12288
MESH = pl.DeviceIdType.MESH


def passed_along(x, axis, by):
    size = lax.axis_size(axis)
    return lax.ppermute(x, axis, [(i, (i + by) % size) for i in range(size)])


def moments(values):
    first_sum, square_sum = lax.psum(
        (jnp.sum(values, axis=1), jnp.sum(values * values, axis=1)), "dp"
    )
    center = first_sum[:, None] / D
    spread = square_sum[:, None] / D - center * center
    return (center, lax.rsqrt(spread + 1e-05))


def normalize(values, ln_gain, ln_bias):
    widened = values.astype(jnp.float32)
    center, inverse = moments(widened)
    return ((widened - center) * inverse * ln_gain + ln_bias).astype(jnp.bfloat16)


def contract(left, weight):
    return lax.dot_general(
        left, weight, (((1,), (1,)), ((), ())), preferred_element_type=jnp.float32
    )


def summed_output(product):
    return lax.psum_scatter(product, "dp", scatter_dimension=0, tiled=True)


def local(section_weights, tensor_inputs, stream_inputs, ln_gain, ln_bias):
    second_section = lax.axis_index("section") == 1
    weight = section_weights[0]
    incoming = tensor_inputs[0]
    saved = stream_inputs[0].astype(jnp.float32)
    partial_sums = jnp.dot(
        lax.all_gather(incoming, "dp", axis=0, tiled=True),
        weight,
        preferred_element_type=jnp.float32,
    )
    summed = lax.psum_scatter(partial_sums, "mp", scatter_dimension=0, tiled=True)
    center, inverse = moments(saved)
    normed = (saved - center) * inverse
    scaled = summed * ln_gain
    first_total, second_total = lax.psum(
        (jnp.sum(scaled, axis=1), jnp.sum(scaled * normed, axis=1)), "dp"
    )
    grad_in = inverse * (scaled - first_total[:, None] / D - normed * (second_total[:, None] / D))
    outgoing = jnp.where(second_section, grad_in, summed + saved).astype(jnp.bfloat16)
    own_rows = passed_along(outgoing, "section", 1)
    operand = jnp.where(second_section, normalize(own_rows, ln_gain, ln_bias), own_rows)
    product = contract(lax.all_gather(operand, "mp", axis=0, tiled=True), weight)
    result = summed_output(product)
    return (own_rows[None], result.astype(jnp.bfloat16)[None])


ARRIVALS = (
    (0, 1, 4, 2, 5, 3, 6, 7),
    (1, 2, 0, 5, 3, 6, 4, 7),
    (2, 1, 3, 6, 0, 5, 7, 4),
    (3, 2, 7, 1, 6, 0, 5, 4),
)
DESTINATIONS = ((3, 2, 1, 0), (3, 2, 0, 1), (0, 1, 3, 2), (0, 1, 2, 3))


def by_place(z, table):
    codes = [sum(entry * 8**i for i, entry in enumerate(row)) for row in table]
    code = jnp.int32(codes[0])
    for place in range(1, 4):
        code = jnp.where(z == place, jnp.int32(codes[place]), code)
    return code


def as_rows(first, second):
    lane = lax.broadcasted_iota(jnp.int32, (128, 128), 1)
    return jnp.where(lane == 0, first, second).T[0:8]


def as_columns(rows):
    square = jnp.concatenate([rows] * 16, axis=0).T
    return square[:, 0:1], square[:, 1:2]


def kernel(
    w_hbm, x_hbm, saved, gain, bias, handed, result,
    w, gath, kept, y_out, y_in, rows, operand, operands, x_in, z_in,
    stat_a, stat_b,
    local_sem, ag_recv, ag_x, ag_up, ag_down, y_send, y_recv,
    a_send, a_recv, b_send, b_recv,
    h_send, h_recv, o_send, o_cross, o_recv, xs_send, xs_recv, zs_send, zs_recv,
):
    s, d, m = lax.axis_index("section"), lax.axis_index("dp"), lax.axis_index("mp")
    z, x = d // 2, d % 2
    first_section = s == 0
    width = w.shape[1]
    depth = w.shape[0]
    f32, bf16 = jnp.float32, jnp.bfloat16

    def block(j, n=1):
        return pl.ds(pl.multiple_of(j * 128, 128), 128 * n)

    def columns(n, size):
        return pl.ds(pl.multiple_of(n * size, size), size)

    def remote(src, dst, send, recv, **where):
        return pltpu.make_async_remote_copy(
            src_ref=src, dst_ref=dst, send_sem=send, recv_sem=recv,
            device_id=where, device_id_type=MESH,
        )

    load_w = pltpu.make_async_copy(w_hbm, w, local_sem.at[0])
    load_x = pltpu.make_async_copy(x_hbm, gath.at[block(d)], local_sem.at[1])
    load_w.start()
    load_x.start()

    barrier = pltpu.get_barrier_semaphore()
    for k in range(1, 8):
        pl.semaphore_signal(barrier, inc=1, device_id={"dp": (d + k) % 8}, device_id_type=MESH)
    pl.semaphore_signal(barrier, inc=1, device_id={"mp": 1 - m}, device_id_type=MESH)
    pl.semaphore_signal(barrier, inc=1, device_id={"section": 1 - s}, device_id_type=MESH)
    pl.semaphore_signal(
        barrier, inc=1, device_id={"section": 1 - s, "mp": 1 - m}, device_id_type=MESH
    )
    pl.semaphore_wait(barrier, 10)
    load_x.wait()

    def over_x(j, zj):
        return remote(gath.at[block(j)], gath.at[block(j)], ag_x.at[zj], ag_recv.at[j], dp=d + 1 - 2 * x)

    def upward(j, zj):
        return remote(gath.at[block(j)], gath.at[block(j)], ag_up.at[zj], ag_recv.at[j], dp=(d + 2) % 8)

    def downward(j, zj):
        return remote(gath.at[block(j)], gath.at[block(j)], ag_down.at[zj], ag_recv.at[j], dp=(d + 6) % 8)

    def y_copy(r):
        return remote(y_out.at[block(r)], y_in.at[block(r)], y_send.at[r], y_recv.at[r], mp=1 - m)

    def send_stats(stats, send, recv, start):
        for k in range(1, 8):
            c = remote(stats.at[d], stats.at[d], send.at[k], recv.at[d], dp=(d + k) % 8)
            if start:
                c.start()
            else:
                c.wait_send()

    def receive_stats(stats, send, recv):
        for k in range(1, 8):
            e = (d + k) % 8
            remote(stats.at[e], stats.at[e], send.at[k], recv.at[e], dp=e).wait_recv()

    def forward(j, zj):
        @pl.when((zj <= z) & (z < 3))
        def _():
            upward(j, zj).start()

        @pl.when((zj >= z) & (z > 0))
        def _():
            downward(j, zj).start()

        over_x(j, zj).start()

    forward(d, z)

    def saved_sums(r, carry):
        v = saved[block(r), :].astype(f32)
        tile = as_rows(
            jnp.sum(v, axis=1, keepdims=True), jnp.sum(v * v, axis=1, keepdims=True)
        )
        stat_a[d, pl.ds(pl.multiple_of(r * 8, 8), 8), :] = tile
        return carry

    lax.fori_loop(0, 4, saved_sums, 0)
    send_stats(stat_a, a_send, a_recv, True)
    load_w.wait()

    def first_product(t, code):
        entry = code % 8
        zj = entry % 4
        same = entry < 4
        j = 2 * zj + jnp.where(same, x, 1 - x)

        @pl.when(t > 0)
        def _():
            remote(
                gath.at[block(j)], gath.at[block(j)], ag_x.at[0], ag_recv.at[j], dp=d + 1 - 2 * x
            ).wait_recv()

            @pl.when(same)
            def _():
                forward(j, zj)

        mine = j // 4 == m
        r = j % 4

        def tile(n, carry):
            part = jnp.dot(
                gath[block(j), :], w[:, columns(n, 256)], preferred_element_type=f32
            )

            @pl.when(mine)
            def _():
                kept[block(r), columns(n, 256)] = part

            @pl.when(jnp.logical_not(mine))
            def _():
                y_out[block(r), columns(n, 256)] = part.astype(bf16)

            return carry

        lax.fori_loop(0, width // 256, tile, 0)

        @pl.when(jnp.logical_not(mine))
        def _():
            y_copy(r).start()

        return code // 8

    lax.fori_loop(0, 8, first_product, by_place(z, ARRIVALS))

    receive_stats(stat_a, a_send, a_recv)
    send_stats(stat_a, a_send, a_recv, False)

    def totals(stats, r):
        at = pl.ds(pl.multiple_of(r * 8, 8), 8)
        total = stats[0, at, :]
        for e in range(1, 8):
            total = total + stats[e, at, :]
        return as_columns(total)

    def moments_of(stats, r):
        first_sum, square_sum = totals(stats, r)
        center = first_sum / D
        spread = square_sum / D - center * center
        return center, lax.rsqrt(spread + 1e-05)

    def section_sums(i, carry):
        r = (i + 2 * m) % 4
        y_copy(r).wait_recv()
        at = pl.ds(pl.multiple_of(r * 8, 8), 8)

        @pl.when(first_section)
        def _():
            v = kept[block(r), :] + y_in[block(r), :].astype(f32) + saved[block(r), :].astype(f32)
            v = v.astype(bf16)
            rows[block(r), :] = v
            v = v.astype(f32)
            stat_b[d, at, :] = as_rows(
                jnp.sum(v, axis=1, keepdims=True), jnp.sum(v * v, axis=1, keepdims=True)
            )

        @pl.when(jnp.logical_not(first_section))
        def _():
            center, inverse = moments_of(stat_a, r)
            scaled = (kept[block(r), :] + y_in[block(r), :].astype(f32)) * gain[...]
            kept[block(r), :] = scaled
            normed = (saved[block(r), :].astype(f32) - center) * inverse
            stat_b[d, at, :] = as_rows(
                jnp.sum(scaled, axis=1, keepdims=True),
                jnp.sum(scaled * normed, axis=1, keepdims=True),
            )

        return carry

    lax.fori_loop(0, 4, section_sums, 0)
    send_stats(stat_b, b_send, b_recv, True)

    def drain(zj, carry):
        j = 2 * zj + x

        @pl.when((zj <= z) & (z < 3))
        def _():
            upward(j, zj).wait_send()

        @pl.when((zj >= z) & (z > 0))
        def _():
            downward(j, zj).wait_send()

        over_x(j, zj).wait_send()
        y_copy(zj).wait_send()
        return carry

    lax.fori_loop(0, 4, drain, 0)
    receive_stats(stat_b, b_send, b_recv)
    send_stats(stat_b, b_send, b_recv, False)

    def operand_near(r):
        b = 4 * m + r
        return remote(
            operand.at[block(r)], operands.at[block(b)], o_send.at[r], o_recv.at[b], section=1 - s
        )

    def operand_far(r):
        b = 4 * m + r
        return remote(
            operand.at[block(r)], operands.at[block(b)], o_cross.at[r], o_recv.at[b],
            section=1 - s, mp=1 - m,
        )

    def hand_over(r):
        return remote(
            rows.at[block(r)], handed.at[block(r)], h_send.at[r], h_recv.at[r], section=1 - s
        )

    def finish_rows(i, carry):
        r = (i + 2 * m) % 4

        @pl.when(first_section)
        def _():
            center, inverse = moments_of(stat_b, r)
            v = rows[block(r), :].astype(f32)
            operand[block(r), :] = ((v - center) * inverse * gain[...] + bias[...]).astype(bf16)

        @pl.when(jnp.logical_not(first_section))
        def _():
            center, inverse = moments_of(stat_a, r)
            first_total, second_total = totals(stat_b, r)
            normed = (saved[block(r), :].astype(f32) - center) * inverse
            v = inverse * (kept[block(r), :] - first_total / D - normed * (second_total / D))
            v = v.astype(bf16)
            rows[block(r), :] = v
            operand[block(r), :] = v

        operand_far(r).start()
        operand_near(r).start()
        return carry

    lax.fori_loop(0, 4, finish_rows, 0)

    def x_copy(zj):
        return remote(
            gath.at[block(2 * zj + 1 - x)], x_in.at[block(zj)], xs_send.at[zj], xs_recv.at[zj],
            dp=d + 1 - 2 * x,
        )

    def second_product(i, code):
        zj = code % 8
        for k in range(2):
            b = 2 * zj + k
            remote(
                operand.at[block(0)], operands.at[block(b)], o_send.at[0], o_recv.at[b],
                section=1 - s,
            ).wait_recv()

        def tile(n, carry):
            part = lax.dot_general(
                operands[block(2 * zj, 2), :], w[columns(n, 256), :],
                (((1,), (1,)), ((), ())), preferred_element_type=f32,
            )
            gath[block(2 * zj, 2), columns(n, 256)] = part.astype(bf16)
            return carry

        lax.fori_loop(0, depth // 256, tile, 0)
        x_copy(zj).start()
        return code // 8

    lax.fori_loop(0, 4, second_product, by_place(z, DESTINATIONS))

    def hand(r, carry):
        hand_over(r).start()
        return carry

    lax.fori_loop(0, 4, hand, 0)

    def z_up(zj):
        return remote(
            x_in.at[block(zj)], z_in.at[block(zj)], zs_send.at[zj], zs_recv.at[zj], dp=(d + 2) % 8
        )

    def z_down(zj):
        slot = jnp.where(zj == z - 1, 4, zj)
        return remote(
            x_in.at[block(zj)], z_in.at[block(slot)], zs_send.at[zj], zs_recv.at[slot], dp=(d + 6) % 8
        )

    def arrived(slot):
        remote(
            x_in.at[block(0)], z_in.at[block(slot)], zs_send.at[0], zs_recv.at[slot], dp=(d + 2) % 8
        ).wait_recv()

    def gather_sums(i, code):
        zj = code % 8
        x_copy(zj).wait_recv()
        own = zj == z
        one = ((zj >= z) & (z > 0)) | ((zj < z) & (z < 3))
        two = own & (z < 3)

        @pl.when(one)
        def _():
            arrived(zj)

        @pl.when(two)
        def _():
            arrived(4)

        def add(with_one, with_two):
            def tile(n, carry):
                c = columns(n, 512)
                total = gath[block(2 * zj + x), c].astype(f32) + x_in[block(zj), c].astype(f32)
                if with_one:
                    total = total + z_in[block(zj), c].astype(f32)
                if with_two:
                    total = total + z_in[block(4), c].astype(f32)
                x_in[block(zj), c] = total.astype(bf16)
                return carry

            lax.fori_loop(0, depth // 512, tile, 0)

        for with_one in (False, True):
            for with_two in (False, True):
                a = one if with_one else jnp.logical_not(one)
                b = two if with_two else jnp.logical_not(two)
                pl.when(a & b)(functools.partial(add, with_one, with_two))

        @pl.when(zj > z)
        def _():
            z_up(zj).start()

        @pl.when(zj < z)
        def _():
            z_down(zj).start()

        return code // 8

    lax.fori_loop(0, 4, gather_sums, by_place(z, DESTINATIONS))
    store = pltpu.make_async_copy(x_in.at[block(z)], result, local_sem.at[2])
    store.start()

    def finish(r, carry):
        hand_over(r).wait()
        operand_near(r).wait_send()
        operand_far(r).wait_send()
        x_copy(r).wait_send()

        @pl.when(r > z)
        def _():
            z_up(r).wait_send()

        @pl.when(r < z)
        def _():
            z_down(r).wait_send()

        return carry

    lax.fori_loop(0, 4, finish, 0)
    store.wait()


def fused_local(section_weights, tensor_inputs, stream_inputs, ln_gain, ln_bias):
    weight = section_weights[0]
    incoming = tensor_inputs[0]
    saved = stream_inputs[0]
    depth, width = weight.shape
    bf16, f32 = jnp.bfloat16, jnp.float32
    sem = pltpu.SemaphoreType.DMA
    anywhere = pl.BlockSpec(memory_space=pl.ANY)
    vmem = pl.BlockSpec(memory_space=pltpu.VMEM)
    handed, result = pl.pallas_call(
        kernel,
        out_shape=(
            jax.ShapeDtypeStruct(saved.shape, bf16),
            jax.ShapeDtypeStruct(incoming.shape, bf16),
        ),
        in_specs=[anywhere, anywhere, vmem, vmem, vmem],
        out_specs=(anywhere, anywhere),
        scratch_shapes=[
            pltpu.VMEM((depth, width), bf16),
            pltpu.VMEM((1024, depth), bf16),
            pltpu.VMEM((512, width), f32),
            pltpu.VMEM((512, width), bf16),
            pltpu.VMEM((512, width), bf16),
            pltpu.VMEM((512, width), bf16),
            pltpu.VMEM((512, width), bf16),
            pltpu.VMEM((1024, width), bf16),
            pltpu.VMEM((512, depth), bf16),
            pltpu.VMEM((640, depth), bf16),
            pltpu.VMEM((8, 32, 128), f32),
            pltpu.VMEM((8, 32, 128), f32),
            sem((3,)), sem((8,)), sem((4,)), sem((4,)), sem((4,)), sem((4,)), sem((4,)),
            sem((8,)), sem((8,)), sem((8,)), sem((8,)),
            sem((4,)), sem((4,)), sem((4,)), sem((4,)), sem((8,)),
            sem((4,)), sem((4,)), sem((4,)), sem((5,)),
        ],
        compiler_params=pltpu.CompilerParams(
            collective_id=0, has_side_effects=True, vmem_limit_bytes=64 * 1024 * 1024 - 65536
        ),
        cost_estimate=pl.CostEstimate(
            flops=4 * 1024 * depth * width, bytes_accessed=2 * depth * width, transcendentals=0
        ),
    )(weight, incoming, saved, ln_gain[None], ln_bias[None])
    return handed[None], result[None]


def solution(mesh):
    fused = dict(mesh.shape) == {"section": 2, "dp": 8, "mp": 2}
    in_specs = (
        P("section", "mp", "dp"),
        P("section", "dp", "mp"),
        P("section", "mp", "dp"),
        P("dp"),
        P("dp"),
    )
    out_specs = (P("section", "mp", "dp"), P("section", "dp", "mp"))
    body = fused_local if fused else local
    return jax.shard_map(body, mesh=mesh, in_specs=in_specs, out_specs=out_specs, check_vma=False)
```

```python
import functools

import jax
import jax.numpy as jnp
from jax import lax
from jax.experimental import pallas as pl
from jax.experimental.pallas import tpu as pltpu
from jax.sharding import PartitionSpec as P

D = 12288
MESH = pl.DeviceIdType.MESH


def passed_along(x, axis, by):
    size = lax.axis_size(axis)
    return lax.ppermute(x, axis, [(i, (i + by) % size) for i in range(size)])


def moments(values):
    first_sum, square_sum = lax.psum(
        (jnp.sum(values, axis=1), jnp.sum(values * values, axis=1)), "dp"
    )
    center = first_sum[:, None] / D
    spread = square_sum[:, None] / D - center * center
    return (center, lax.rsqrt(spread + 1e-05))


def normalize(values, ln_gain, ln_bias):
    widened = values.astype(jnp.float32)
    center, inverse = moments(widened)
    return ((widened - center) * inverse * ln_gain + ln_bias).astype(jnp.bfloat16)


def contract(left, weight):
    return lax.dot_general(
        left, weight, (((1,), (1,)), ((), ())), preferred_element_type=jnp.float32
    )


def summed_output(product):
    return lax.psum_scatter(product, "dp", scatter_dimension=0, tiled=True)


def local(section_weights, tensor_inputs, stream_inputs, ln_gain, ln_bias):
    second_section = lax.axis_index("section") == 1
    weight = section_weights[0]
    incoming = tensor_inputs[0]
    saved = stream_inputs[0].astype(jnp.float32)
    partial_sums = jnp.dot(
        lax.all_gather(incoming, "dp", axis=0, tiled=True),
        weight,
        preferred_element_type=jnp.float32,
    )
    summed = lax.psum_scatter(partial_sums, "mp", scatter_dimension=0, tiled=True)
    center, inverse = moments(saved)
    normed = (saved - center) * inverse
    scaled = summed * ln_gain
    first_total, second_total = lax.psum(
        (jnp.sum(scaled, axis=1), jnp.sum(scaled * normed, axis=1)), "dp"
    )
    grad_in = inverse * (scaled - first_total[:, None] / D - normed * (second_total[:, None] / D))
    outgoing = jnp.where(second_section, grad_in, summed + saved).astype(jnp.bfloat16)
    own_rows = passed_along(outgoing, "section", 1)
    operand = jnp.where(second_section, normalize(own_rows, ln_gain, ln_bias), own_rows)
    product = contract(lax.all_gather(operand, "mp", axis=0, tiled=True), weight)
    result = summed_output(product)
    return (own_rows[None], result.astype(jnp.bfloat16)[None])


ARRIVALS = (
    (0, 1, 4, 2, 5, 3, 6, 7),
    (1, 2, 0, 5, 3, 6, 4, 7),
    (2, 1, 3, 6, 0, 5, 7, 4),
    (3, 2, 7, 1, 6, 0, 5, 4),
)
DESTINATIONS = ((3, 2, 1, 0), (3, 2, 0, 1), (0, 1, 3, 2), (0, 1, 2, 3))


def by_place(z, table):
    codes = [sum(entry * 8**i for i, entry in enumerate(row)) for row in table]
    code = jnp.int32(codes[0])
    for place in range(1, 4):
        code = jnp.where(z == place, jnp.int32(codes[place]), code)
    return code


def as_rows(first, second):
    lane = lax.broadcasted_iota(jnp.int32, (128, 128), 1)
    return jnp.where(lane == 0, first, second).T[0:8]


def as_columns(rows):
    square = jnp.concatenate([rows] * 16, axis=0).T
    return square[:, 0:1], square[:, 1:2]


def kernel(
    w_hbm, x_hbm, saved, gain, bias, handed, result,
    w, gath, kept, y_out, y_in, rows, operand, operands, x_in, z_in,
    zb_in, stat_a, stat_b,
    local_sem, ag_recv, ag_x, ag_up, ag_down, y_send, y_recv,
    a_send, a_recv, b_send, b_recv,
    h_send, h_recv, o_send, o_cross, o_recv, xs_send, xs_recv, zs_send, zs_recv,
    ab_send, ab_recv, zb_send, zb_recv,
):
    s, d, m = lax.axis_index("section"), lax.axis_index("dp"), lax.axis_index("mp")
    z, x = d // 2, d % 2
    first_section = s == 0
    width = w.shape[1]
    depth = w.shape[0]
    f32, bf16 = jnp.float32, jnp.bfloat16

    def block(j, n=1):
        return pl.ds(pl.multiple_of(j * 128, 128), 128 * n)

    def half(j, h):
        return pl.ds(pl.multiple_of(j * 128 + h * 64, 64), 64)

    def is_edge(zj):
        return (zj == 0) | (zj == 3)

    def is_split(zj):
        return is_edge(zj) & (zj != z)

    def columns(n, size):
        return pl.ds(pl.multiple_of(n * size, size), size)

    def remote(src, dst, send, recv, **where):
        return pltpu.make_async_remote_copy(
            src_ref=src, dst_ref=dst, send_sem=send, recv_sem=recv,
            device_id=where, device_id_type=MESH,
        )

    load_w = pltpu.make_async_copy(w_hbm, w, local_sem.at[0])
    load_x = pltpu.make_async_copy(x_hbm, gath.at[block(d)], local_sem.at[1])
    load_w.start()
    load_x.start()

    barrier = pltpu.get_barrier_semaphore()
    for k in range(1, 8):
        pl.semaphore_signal(barrier, inc=1, device_id={"dp": (d + k) % 8}, device_id_type=MESH)
    pl.semaphore_signal(barrier, inc=1, device_id={"mp": 1 - m}, device_id_type=MESH)
    pl.semaphore_signal(barrier, inc=1, device_id={"section": 1 - s}, device_id_type=MESH)
    pl.semaphore_signal(
        barrier, inc=1, device_id={"section": 1 - s, "mp": 1 - m}, device_id_type=MESH
    )
    pl.semaphore_wait(barrier, 10)
    load_x.wait()

    def over_x(j, zj, at):
        return remote(gath.at[at], gath.at[at], ag_x.at[zj], ag_recv.at[j], dp=d + 1 - 2 * x)

    def whole_or_half(zj, j, act):
        pl.when(is_split(zj))(lambda: act(half(j, 0)))
        pl.when(jnp.logical_not(is_split(zj)))(lambda: act(block(j)))

    def half_along_z(j, e, act):
        def go(target):
            act(remote(gath.at[half(j, 1)], gath.at[half(j, 1)], ab_send.at[e], ab_recv.at[e], dp=target))

        pl.when((e == 0) & (z < 3))(lambda: go((d + 2) % 8))
        pl.when((e == 1) & (z > 0))(lambda: go((d + 6) % 8))

    def upward(j, zj):
        return remote(gath.at[block(j)], gath.at[block(j)], ag_up.at[zj], ag_recv.at[j], dp=(d + 2) % 8)

    def downward(j, zj):
        return remote(gath.at[block(j)], gath.at[block(j)], ag_down.at[zj], ag_recv.at[j], dp=(d + 6) % 8)

    def y_copy(r):
        return remote(y_out.at[block(r)], y_in.at[block(r)], y_send.at[r], y_recv.at[r], mp=1 - m)

    def send_stats(stats, send, recv, start):
        for k in range(1, 8):
            c = remote(stats.at[d], stats.at[d], send.at[k], recv.at[d], dp=(d + k) % 8)
            if start:
                c.start()
            else:
                c.wait_send()

    def receive_stats(stats, send, recv):
        for k in range(1, 8):
            e = (d + k) % 8
            remote(stats.at[e], stats.at[e], send.at[k], recv.at[e], dp=e).wait_recv()

    def forward(j, zj):
        @pl.when((zj <= z) & (z < 3))
        def _():
            upward(j, zj).start()

        @pl.when((zj >= z) & (z > 0))
        def _():
            downward(j, zj).start()

        whole_or_half(zj, j, lambda at: over_x(j, zj, at).start())

    forward(d, z)

    def saved_sums(r, carry):
        v = saved[block(r), :].astype(f32)
        tile = as_rows(
            jnp.sum(v, axis=1, keepdims=True), jnp.sum(v * v, axis=1, keepdims=True)
        )
        stat_a[d, pl.ds(pl.multiple_of(r * 8, 8), 8), :] = tile
        return carry

    lax.fori_loop(0, 4, saved_sums, 0)
    send_stats(stat_a, a_send, a_recv, True)
    load_w.wait()

    def first_product(t, code):
        entry = code % 8
        zj = entry % 4
        same = entry < 4
        j = 2 * zj + jnp.where(same, x, 1 - x)

        other = jnp.logical_not(same)
        parted = other & is_split(zj)
        e = zj // 3

        @pl.when((t > 0) & jnp.logical_not(parted))
        def _():
            over_x(j, zj, block(j)).wait_recv()

            @pl.when(same)
            def _():
                forward(j, zj)

        @pl.when(parted)
        def _():
            remote(
                gath.at[half(j, 1)], gath.at[half(j, 1)], ab_send.at[e], ab_recv.at[e], dp=(d + 2) % 8
            ).wait_recv()

        @pl.when(other & is_edge(zj))
        def _():
            half_along_z(j, e, lambda c: c.start())

        @pl.when(parted)
        def _():
            over_x(j, zj, half(j, 0)).wait_recv()

        mine = j // 4 == m
        r = j % 4

        def tile(n, carry):
            part = jnp.dot(
                gath[block(j), :], w[:, columns(n, 256)], preferred_element_type=f32
            )

            @pl.when(mine)
            def _():
                kept[block(r), columns(n, 256)] = part

            @pl.when(jnp.logical_not(mine))
            def _():
                y_out[block(r), columns(n, 256)] = part.astype(bf16)

            return carry

        lax.fori_loop(0, width // 256, tile, 0)

        @pl.when(jnp.logical_not(mine))
        def _():
            y_copy(r).start()

        return code // 8

    lax.fori_loop(0, 8, first_product, by_place(z, ARRIVALS))

    receive_stats(stat_a, a_send, a_recv)
    send_stats(stat_a, a_send, a_recv, False)

    def totals(stats, r):
        at = pl.ds(pl.multiple_of(r * 8, 8), 8)
        total = stats[0, at, :]
        for e in range(1, 8):
            total = total + stats[e, at, :]
        return as_columns(total)

    def moments_of(stats, r):
        first_sum, square_sum = totals(stats, r)
        center = first_sum / D
        spread = square_sum / D - center * center
        return center, lax.rsqrt(spread + 1e-05)

    def section_sums(i, carry):
        r = (i + 2 * m) % 4
        y_copy(r).wait_recv()
        at = pl.ds(pl.multiple_of(r * 8, 8), 8)

        @pl.when(first_section)
        def _():
            v = kept[block(r), :] + y_in[block(r), :].astype(f32) + saved[block(r), :].astype(f32)
            v = v.astype(bf16)
            rows[block(r), :] = v
            v = v.astype(f32)
            stat_b[d, at, :] = as_rows(
                jnp.sum(v, axis=1, keepdims=True), jnp.sum(v * v, axis=1, keepdims=True)
            )

        @pl.when(jnp.logical_not(first_section))
        def _():
            center, inverse = moments_of(stat_a, r)
            scaled = (kept[block(r), :] + y_in[block(r), :].astype(f32)) * gain[...]
            kept[block(r), :] = scaled
            normed = (saved[block(r), :].astype(f32) - center) * inverse
            stat_b[d, at, :] = as_rows(
                jnp.sum(scaled, axis=1, keepdims=True),
                jnp.sum(scaled * normed, axis=1, keepdims=True),
            )

        return carry

    lax.fori_loop(0, 4, section_sums, 0)
    send_stats(stat_b, b_send, b_recv, True)

    def drain(zj, carry):
        j = 2 * zj + x

        @pl.when((zj <= z) & (z < 3))
        def _():
            upward(j, zj).wait_send()

        @pl.when((zj >= z) & (z > 0))
        def _():
            downward(j, zj).wait_send()

        whole_or_half(zj, j, lambda at: over_x(j, zj, at).wait_send())

        @pl.when(is_edge(zj))
        def _():
            half_along_z(2 * zj + 1 - x, zj // 3, lambda c: c.wait_send())

        y_copy(zj).wait_send()
        return carry

    lax.fori_loop(0, 4, drain, 0)
    receive_stats(stat_b, b_send, b_recv)
    send_stats(stat_b, b_send, b_recv, False)

    def operand_near(r):
        b = 4 * m + r
        return remote(
            operand.at[block(r)], operands.at[block(b)], o_send.at[r], o_recv.at[b], section=1 - s
        )

    def operand_far(r):
        b = 4 * m + r
        return remote(
            operand.at[block(r)], operands.at[block(b)], o_cross.at[r], o_recv.at[b],
            section=1 - s, mp=1 - m,
        )

    def hand_over(r):
        return remote(
            rows.at[block(r)], handed.at[block(r)], h_send.at[r], h_recv.at[r], section=1 - s
        )

    def finish_rows(i, carry):
        r = (i + 2 * m) % 4

        @pl.when(first_section)
        def _():
            center, inverse = moments_of(stat_b, r)
            v = rows[block(r), :].astype(f32)
            operand[block(r), :] = ((v - center) * inverse * gain[...] + bias[...]).astype(bf16)

        @pl.when(jnp.logical_not(first_section))
        def _():
            center, inverse = moments_of(stat_a, r)
            first_total, second_total = totals(stat_b, r)
            normed = (saved[block(r), :].astype(f32) - center) * inverse
            v = inverse * (kept[block(r), :] - first_total / D - normed * (second_total / D))
            v = v.astype(bf16)
            rows[block(r), :] = v
            operand[block(r), :] = v

        operand_far(r).start()
        operand_near(r).start()
        return carry

    lax.fori_loop(0, 4, finish_rows, 0)

    def x_copy(zj, act):
        def go(source, target):
            act(
                remote(
                    gath.at[source], x_in.at[target], xs_send.at[zj], xs_recv.at[zj],
                    dp=d + 1 - 2 * x,
                )
            )

        j = 2 * zj + 1 - x
        pl.when(is_split(zj))(lambda: go(half(j, 0), half(zj, 0)))
        pl.when(jnp.logical_not(is_split(zj)))(lambda: go(block(j), block(zj)))

    def half_sums(e, act):
        def go(target):
            act(
                remote(
                    gath.at[half(6 * e + 1 - x, 1)], zb_in.at[half(0, e)], zb_send.at[e],
                    zb_recv.at[e], dp=target,
                )
            )

        pl.when((e == 1) & (z < 3))(lambda: go((d + 2) % 8))
        pl.when((e == 0) & (z > 0))(lambda: go((d + 6) % 8))

    def add_half(e):
        j = 6 * e + 1 - x
        remote(
            gath.at[half(j, 1)], zb_in.at[half(0, e)], zb_send.at[e], zb_recv.at[e], dp=(d + 2) % 8
        ).wait_recv()

        def tile(n, carry):
            c = columns(n, 512)
            total = gath[half(j, 1), c].astype(f32) + zb_in[half(0, e), c].astype(f32)
            gath[half(j, 1), c] = total.astype(bf16)
            return carry

        lax.fori_loop(0, depth // 512, tile, 0)

    def second_product(i, code):
        zj = code % 8
        for k in range(2):
            b = 2 * zj + k
            remote(
                operand.at[block(0)], operands.at[block(b)], o_send.at[0], o_recv.at[b],
                section=1 - s,
            ).wait_recv()

        def tile(n, carry):
            part = lax.dot_general(
                operands[block(2 * zj, 2), :], w[columns(n, 256), :],
                (((1,), (1,)), ((), ())), preferred_element_type=f32,
            )
            gath[block(2 * zj, 2), columns(n, 256)] = part.astype(bf16)
            return carry

        lax.fori_loop(0, depth // 256, tile, 0)
        @pl.when(is_split(zj) & is_edge(z))
        def _():
            half_sums(zj // 3, lambda c: c.start())

        @pl.when(jnp.logical_not(is_edge(zj) & (zj == z)))
        def _():
            x_copy(zj, lambda c: c.start())

        return code // 8

    lax.fori_loop(0, 4, second_product, by_place(z, DESTINATIONS))

    @pl.when(jnp.logical_not(is_edge(z)))
    def _():
        def pass_on(i, carry):
            e = (i + z) % 2
            add_half(e)
            half_sums(e, lambda c: c.start())
            return carry

        lax.fori_loop(0, 2, pass_on, 0)

    def hand(r, carry):
        hand_over(r).start()
        return carry

    lax.fori_loop(0, 4, hand, 0)

    def z_up(zj):
        return remote(
            x_in.at[block(zj)], z_in.at[block(zj)], zs_send.at[zj], zs_recv.at[zj], dp=(d + 2) % 8
        )

    def z_down(zj):
        slot = jnp.where(zj == z - 1, 4, zj)
        return remote(
            x_in.at[block(zj)], z_in.at[block(slot)], zs_send.at[zj], zs_recv.at[slot], dp=(d + 6) % 8
        )

    def arrived(slot):
        remote(
            x_in.at[block(0)], z_in.at[block(slot)], zs_send.at[0], zs_recv.at[slot], dp=(d + 2) % 8
        ).wait_recv()

    def gather_sums(i, code):
        zj = code % 8

        @pl.when((i == 2) & is_edge(z))
        def _():
            add_half(z // 3)
            x_copy(z, lambda c: c.start())

        x_copy(zj, lambda c: c.wait_recv())
        own = zj == z
        one = ((zj >= z) & (z > 0)) | ((zj < z) & (z < 3))
        two = own & (z < 3)

        @pl.when(one)
        def _():
            arrived(zj)

        @pl.when(two)
        def _():
            arrived(4)

        def add(h, with_x, with_one, with_two):
            def tile(n, carry):
                c = columns(n, 512)
                total = gath[half(2 * zj + x, h), c].astype(f32)
                if with_x:
                    total = total + x_in[half(zj, h), c].astype(f32)
                if with_one:
                    total = total + z_in[half(zj, h), c].astype(f32)
                if with_two:
                    total = total + z_in[half(4, h), c].astype(f32)
                x_in[half(zj, h), c] = total.astype(bf16)
                return carry

            lax.fori_loop(0, depth // 512, tile, 0)

        for with_one in (False, True):
            for with_two in (False, True):
                a = one if with_one else jnp.logical_not(one)
                b = two if with_two else jnp.logical_not(two)
                pl.when(a & b)(functools.partial(add, 0, True, with_one, with_two))
                for with_x in (False, True):
                    if with_x or not with_two:
                        c = jnp.logical_not(is_split(zj)) if with_x else is_split(zj)
                        pl.when(a & b & c)(functools.partial(add, 1, with_x, with_one, with_two))

        @pl.when(zj > z)
        def _():
            z_up(zj).start()

        @pl.when(zj < z)
        def _():
            z_down(zj).start()

        return code // 8

    lax.fori_loop(0, 4, gather_sums, by_place(z, DESTINATIONS))
    store = pltpu.make_async_copy(x_in.at[block(z)], result, local_sem.at[2])
    store.start()

    def finish(r, carry):
        hand_over(r).wait()
        operand_near(r).wait_send()
        operand_far(r).wait_send()
        x_copy(r, lambda c: c.wait_send())

        @pl.when(r < 2)
        def _():
            half_sums(r, lambda c: c.wait_send())

        @pl.when(r > z)
        def _():
            z_up(r).wait_send()

        @pl.when(r < z)
        def _():
            z_down(r).wait_send()

        return carry

    lax.fori_loop(0, 4, finish, 0)
    store.wait()


def fused_local(section_weights, tensor_inputs, stream_inputs, ln_gain, ln_bias):
    weight = section_weights[0]
    incoming = tensor_inputs[0]
    saved = stream_inputs[0]
    depth, width = weight.shape
    bf16, f32 = jnp.bfloat16, jnp.float32
    sem = pltpu.SemaphoreType.DMA
    anywhere = pl.BlockSpec(memory_space=pl.ANY)
    vmem = pl.BlockSpec(memory_space=pltpu.VMEM)
    handed, result = pl.pallas_call(
        kernel,
        out_shape=(
            jax.ShapeDtypeStruct(saved.shape, bf16),
            jax.ShapeDtypeStruct(incoming.shape, bf16),
        ),
        in_specs=[anywhere, anywhere, vmem, vmem, vmem],
        out_specs=(anywhere, anywhere),
        scratch_shapes=[
            pltpu.VMEM((depth, width), bf16),
            pltpu.VMEM((1024, depth), bf16),
            pltpu.VMEM((512, width), f32),
            pltpu.VMEM((512, width), bf16),
            pltpu.VMEM((512, width), bf16),
            pltpu.VMEM((512, width), bf16),
            pltpu.VMEM((512, width), bf16),
            pltpu.VMEM((1024, width), bf16),
            pltpu.VMEM((512, depth), bf16),
            pltpu.VMEM((640, depth), bf16),
            pltpu.VMEM((128, depth), bf16),
            pltpu.VMEM((8, 32, 128), f32),
            pltpu.VMEM((8, 32, 128), f32),
            sem((3,)), sem((8,)), sem((4,)), sem((4,)), sem((4,)), sem((4,)), sem((4,)),
            sem((8,)), sem((8,)), sem((8,)), sem((8,)),
            sem((4,)), sem((4,)), sem((4,)), sem((4,)), sem((8,)),
            sem((4,)), sem((4,)), sem((4,)), sem((5,)),
            sem((2,)), sem((2,)), sem((2,)), sem((2,)),
        ],
        compiler_params=pltpu.CompilerParams(
            collective_id=0, has_side_effects=True, vmem_limit_bytes=64 * 1024 * 1024 - 65536
        ),
        cost_estimate=pl.CostEstimate(
            flops=4 * 1024 * depth * width, bytes_accessed=2 * depth * width, transcendentals=0
        ),
    )(weight, incoming, saved, ln_gain[None], ln_bias[None])
    return handed[None], result[None]


def solution(mesh):
    fused = dict(mesh.shape) == {"section": 2, "dp": 8, "mp": 2}
    in_specs = (
        P("section", "mp", "dp"),
        P("section", "dp", "mp"),
        P("section", "mp", "dp"),
        P("dp"),
        P("dp"),
    )
    out_specs = (P("section", "mp", "dp"), P("section", "dp", "mp"))
    body = fused_local if fused else local
    return jax.shard_map(body, mesh=mesh, in_specs=in_specs, out_specs=out_specs, check_vma=False)
```

```python
import functools

import jax
import jax.numpy as jnp
from jax import lax
from jax.experimental import pallas as pl
from jax.experimental.pallas import tpu as pltpu
from jax.sharding import PartitionSpec as P

D = 12288
MESH = pl.DeviceIdType.MESH


def passed_along(x, axis, by):
    size = lax.axis_size(axis)
    return lax.ppermute(x, axis, [(i, (i + by) % size) for i in range(size)])


def moments(values):
    first_sum, square_sum = lax.psum(
        (jnp.sum(values, axis=1), jnp.sum(values * values, axis=1)), "dp"
    )
    center = first_sum[:, None] / D
    spread = square_sum[:, None] / D - center * center
    return (center, lax.rsqrt(spread + 1e-05))


def normalize(values, ln_gain, ln_bias):
    widened = values.astype(jnp.float32)
    center, inverse = moments(widened)
    return ((widened - center) * inverse * ln_gain + ln_bias).astype(jnp.bfloat16)


def contract(left, weight):
    return lax.dot_general(
        left, weight, (((1,), (1,)), ((), ())), preferred_element_type=jnp.float32
    )


def summed_output(product):
    return lax.psum_scatter(product, "dp", scatter_dimension=0, tiled=True)


def local(section_weights, tensor_inputs, stream_inputs, ln_gain, ln_bias):
    second_section = lax.axis_index("section") == 1
    weight = section_weights[0]
    incoming = tensor_inputs[0]
    saved = stream_inputs[0].astype(jnp.float32)
    partial_sums = jnp.dot(
        lax.all_gather(incoming, "dp", axis=0, tiled=True),
        weight,
        preferred_element_type=jnp.float32,
    )
    summed = lax.psum_scatter(partial_sums, "mp", scatter_dimension=0, tiled=True)
    center, inverse = moments(saved)
    normed = (saved - center) * inverse
    scaled = summed * ln_gain
    first_total, second_total = lax.psum(
        (jnp.sum(scaled, axis=1), jnp.sum(scaled * normed, axis=1)), "dp"
    )
    grad_in = inverse * (scaled - first_total[:, None] / D - normed * (second_total[:, None] / D))
    outgoing = jnp.where(second_section, grad_in, summed + saved).astype(jnp.bfloat16)
    own_rows = passed_along(outgoing, "section", 1)
    operand = jnp.where(second_section, normalize(own_rows, ln_gain, ln_bias), own_rows)
    product = contract(lax.all_gather(operand, "mp", axis=0, tiled=True), weight)
    result = summed_output(product)
    return (own_rows[None], result.astype(jnp.bfloat16)[None])


ARRIVALS = (
    (0, 1, 4, 2, 5, 3, 6, 7),
    (1, 2, 0, 5, 3, 6, 4, 7),
    (2, 1, 3, 6, 0, 5, 7, 4),
    (3, 2, 7, 1, 6, 0, 5, 4),
)
DESTINATIONS = ((3, 2, 1, 0), (3, 2, 0, 1), (0, 1, 3, 2), (0, 1, 2, 3))


def by_place(z, table):
    codes = [sum(entry * 8**i for i, entry in enumerate(row)) for row in table]
    code = jnp.int32(codes[0])
    for place in range(1, 4):
        code = jnp.where(z == place, jnp.int32(codes[place]), code)
    return code


def as_rows(first, second):
    lane = lax.broadcasted_iota(jnp.int32, (128, 128), 1)
    return jnp.where(lane == 0, first, second).T[0:8]


def as_columns(rows):
    square = jnp.concatenate([rows] * 16, axis=0).T
    return square[:, 0:1], square[:, 1:2]


def kernel(
    w_hbm, x_hbm, saved, gain, bias, handed, result,
    w, gath, kept, y_out, y_in, rows, operand, operands, x_in, z_in,
    zb_in, stat_a, stat_b,
    local_sem, ag_recv, ag_x, ag_up, ag_down, y_send, y_recv,
    a_send, a_recv, b_send, b_recv,
    h_send, h_recv, o_send, o_cross, o_recv, xs_send, xs_recv, zs_send, zs_recv,
    ab_send, ab_recv, zb_send, zb_recv,
):
    s, d, m = lax.axis_index("section"), lax.axis_index("dp"), lax.axis_index("mp")
    z, x = d // 2, d % 2
    first_section = s == 0
    width = w.shape[1]
    depth = w.shape[0]
    f32, bf16 = jnp.float32, jnp.bfloat16

    def block(j, n=1):
        return pl.ds(pl.multiple_of(j * 128, 128), 128 * n)

    def half(j, h):
        return pl.ds(pl.multiple_of(j * 128 + h * 64, 64), 64)

    def is_edge(zj):
        return (zj == 0) | (zj == 3)

    def is_split(zj):
        return is_edge(zj) & (zj != z)

    def columns(n, size):
        return pl.ds(pl.multiple_of(n * size, size), size)

    def remote(src, dst, send, recv, **where):
        return pltpu.make_async_remote_copy(
            src_ref=src, dst_ref=dst, send_sem=send, recv_sem=recv,
            device_id=where, device_id_type=MESH,
        )

    load_w = pltpu.make_async_copy(w_hbm, w, local_sem.at[0])
    load_x = pltpu.make_async_copy(x_hbm, gath.at[block(d)], local_sem.at[1])
    load_w.start()
    load_x.start()

    barrier = pltpu.get_barrier_semaphore()
    for k in range(1, 8):
        pl.semaphore_signal(barrier, inc=1, device_id={"dp": (d + k) % 8}, device_id_type=MESH)
    pl.semaphore_signal(barrier, inc=1, device_id={"mp": 1 - m}, device_id_type=MESH)
    pl.semaphore_signal(barrier, inc=1, device_id={"section": 1 - s}, device_id_type=MESH)
    pl.semaphore_signal(
        barrier, inc=1, device_id={"section": 1 - s, "mp": 1 - m}, device_id_type=MESH
    )
    pl.semaphore_wait(barrier, 10)
    load_x.wait()

    def over_x(j, zj, at):
        return remote(gath.at[at], gath.at[at], ag_x.at[zj], ag_recv.at[j], dp=d + 1 - 2 * x)

    def whole_or_half(zj, j, act):
        pl.when(is_split(zj))(lambda: act(half(j, 0)))
        pl.when(jnp.logical_not(is_split(zj)))(lambda: act(block(j)))

    def half_along_z(j, e, act):
        def go(target):
            act(remote(gath.at[half(j, 1)], gath.at[half(j, 1)], ab_send.at[e], ab_recv.at[e], dp=target))

        pl.when((e == 0) & (z < 3))(lambda: go((d + 2) % 8))
        pl.when((e == 1) & (z > 0))(lambda: go((d + 6) % 8))

    def upward(j, zj):
        return remote(gath.at[block(j)], gath.at[block(j)], ag_up.at[zj], ag_recv.at[j], dp=(d + 2) % 8)

    def downward(j, zj):
        return remote(gath.at[block(j)], gath.at[block(j)], ag_down.at[zj], ag_recv.at[j], dp=(d + 6) % 8)

    def y_copy(r):
        return remote(y_out.at[block(r)], y_in.at[block(r)], y_send.at[r], y_recv.at[r], mp=1 - m)

    def send_stats(stats, send, recv, start):
        for k in range(1, 8):
            c = remote(stats.at[d], stats.at[d], send.at[k], recv.at[d], dp=(d + k) % 8)
            if start:
                c.start()
            else:
                c.wait_send()

    def receive_stats(stats, send, recv):
        for k in range(1, 8):
            e = (d + k) % 8
            remote(stats.at[e], stats.at[e], send.at[k], recv.at[e], dp=e).wait_recv()

    def forward(j, zj):
        @pl.when((zj <= z) & (z < 3))
        def _():
            upward(j, zj).start()

        @pl.when((zj >= z) & (z > 0))
        def _():
            downward(j, zj).start()

        whole_or_half(zj, j, lambda at: over_x(j, zj, at).start())

    forward(d, z)

    def saved_sums(r, carry):
        v = saved[block(r), :].astype(f32)
        tile = as_rows(
            jnp.sum(v, axis=1, keepdims=True), jnp.sum(v * v, axis=1, keepdims=True)
        )
        stat_a[d, pl.ds(pl.multiple_of(r * 8, 8), 8), :] = tile
        return carry

    lax.fori_loop(0, 4, saved_sums, 0)
    send_stats(stat_a, a_send, a_recv, True)
    load_w.wait()

    def first_product(t, code):
        entry = code % 8
        zj = entry % 4
        same = entry < 4
        j = 2 * zj + jnp.where(same, x, 1 - x)

        other = jnp.logical_not(same)
        parted = other & is_split(zj)
        e = zj // 3

        @pl.when((t > 0) & jnp.logical_not(parted))
        def _():
            over_x(j, zj, block(j)).wait_recv()

            @pl.when(same)
            def _():
                forward(j, zj)

        @pl.when(parted)
        def _():
            remote(
                gath.at[half(j, 1)], gath.at[half(j, 1)], ab_send.at[e], ab_recv.at[e], dp=(d + 2) % 8
            ).wait_recv()

        @pl.when(other & is_edge(zj))
        def _():
            half_along_z(j, e, lambda c: c.start())

        @pl.when(parted)
        def _():
            over_x(j, zj, half(j, 0)).wait_recv()

        mine = j // 4 == m
        r = j % 4

        def tile(n, carry):
            part = jnp.dot(
                gath[block(j), :], w[:, columns(n, 256)], preferred_element_type=f32
            )

            @pl.when(mine)
            def _():
                kept[block(r), columns(n, 256)] = part

            @pl.when(jnp.logical_not(mine))
            def _():
                y_out[block(r), columns(n, 256)] = part.astype(bf16)

            return carry

        lax.fori_loop(0, width // 256, tile, 0)

        @pl.when(jnp.logical_not(mine))
        def _():
            y_copy(r).start()

        return code // 8

    lax.fori_loop(0, 8, first_product, by_place(z, ARRIVALS))

    receive_stats(stat_a, a_send, a_recv)
    send_stats(stat_a, a_send, a_recv, False)

    def totals(stats, r):
        at = pl.ds(pl.multiple_of(r * 8, 8), 8)
        total = stats[0, at, :]
        for e in range(1, 8):
            total = total + stats[e, at, :]
        return as_columns(total)

    def moments_of(stats, r):
        first_sum, square_sum = totals(stats, r)
        center = first_sum / D
        spread = square_sum / D - center * center
        return center, lax.rsqrt(spread + 1e-05)

    def section_sums(i, carry):
        r = (i + 2 * m) % 4
        y_copy(r).wait_recv()
        at = pl.ds(pl.multiple_of(r * 8, 8), 8)

        @pl.when(first_section)
        def _():
            v = kept[block(r), :] + y_in[block(r), :].astype(f32) + saved[block(r), :].astype(f32)
            v = v.astype(bf16)
            rows[block(r), :] = v
            v = v.astype(f32)
            stat_b[d, at, :] = as_rows(
                jnp.sum(v, axis=1, keepdims=True), jnp.sum(v * v, axis=1, keepdims=True)
            )

        @pl.when(jnp.logical_not(first_section))
        def _():
            center, inverse = moments_of(stat_a, r)
            scaled = (kept[block(r), :] + y_in[block(r), :].astype(f32)) * gain[...]
            kept[block(r), :] = scaled
            normed = (saved[block(r), :].astype(f32) - center) * inverse
            stat_b[d, at, :] = as_rows(
                jnp.sum(scaled, axis=1, keepdims=True),
                jnp.sum(scaled * normed, axis=1, keepdims=True),
            )

        return carry

    lax.fori_loop(0, 4, section_sums, 0)
    send_stats(stat_b, b_send, b_recv, True)

    def drain(zj, carry):
        j = 2 * zj + x

        @pl.when((zj <= z) & (z < 3))
        def _():
            upward(j, zj).wait_send()

        @pl.when((zj >= z) & (z > 0))
        def _():
            downward(j, zj).wait_send()

        whole_or_half(zj, j, lambda at: over_x(j, zj, at).wait_send())

        @pl.when(is_edge(zj))
        def _():
            half_along_z(2 * zj + 1 - x, zj // 3, lambda c: c.wait_send())

        y_copy(zj).wait_send()
        return carry

    lax.fori_loop(0, 4, drain, 0)
    receive_stats(stat_b, b_send, b_recv)
    send_stats(stat_b, b_send, b_recv, False)

    def operand_near(r):
        b = 4 * m + r
        return remote(
            operand.at[block(r)], operands.at[block(b)], o_send.at[r], o_recv.at[b], section=1 - s
        )

    def operand_far(r):
        b = 4 * m + r
        return remote(
            operand.at[block(r)], operands.at[block(b)], o_cross.at[r], o_recv.at[b],
            section=1 - s, mp=1 - m,
        )

    def hand_over(r):
        return remote(
            rows.at[block(r)], handed.at[block(r)], h_send.at[r], h_recv.at[r], section=1 - s
        )

    def finish_rows(i, carry):
        r = 2 * ((i // 2 + m) % 2) + 1 - x + (i % 2) * (2 * x - 1)

        @pl.when(first_section)
        def _():
            center, inverse = moments_of(stat_b, r)
            v = rows[block(r), :].astype(f32)
            operand[block(r), :] = ((v - center) * inverse * gain[...] + bias[...]).astype(bf16)

        @pl.when(jnp.logical_not(first_section))
        def _():
            center, inverse = moments_of(stat_a, r)
            first_total, second_total = totals(stat_b, r)
            normed = (saved[block(r), :].astype(f32) - center) * inverse
            v = inverse * (kept[block(r), :] - first_total / D - normed * (second_total / D))
            v = v.astype(bf16)
            rows[block(r), :] = v
            operand[block(r), :] = v

        operand_far(r).start()
        operand_near(r).start()
        return carry

    lax.fori_loop(0, 4, finish_rows, 0)

    def x_copy(zj, act):
        def go(source, target):
            act(
                remote(
                    gath.at[source], x_in.at[target], xs_send.at[zj], xs_recv.at[zj],
                    dp=d + 1 - 2 * x,
                )
            )

        j = 2 * zj + 1 - x
        pl.when(is_split(zj))(lambda: go(half(j, 0), half(zj, 0)))
        pl.when(jnp.logical_not(is_split(zj)))(lambda: go(block(j), block(zj)))

    def half_sums(e, act):
        def go(target):
            act(
                remote(
                    gath.at[half(6 * e + 1 - x, 1)], zb_in.at[half(0, e)], zb_send.at[e],
                    zb_recv.at[e], dp=target,
                )
            )

        pl.when((e == 1) & (z < 3))(lambda: go((d + 2) % 8))
        pl.when((e == 0) & (z > 0))(lambda: go((d + 6) % 8))

    def add_half(e):
        j = 6 * e + 1 - x
        remote(
            gath.at[half(j, 1)], zb_in.at[half(0, e)], zb_send.at[e], zb_recv.at[e], dp=(d + 2) % 8
        ).wait_recv()

        def tile(n, carry):
            c = columns(n, 512)
            total = gath[half(j, 1), c].astype(f32) + zb_in[half(0, e), c].astype(f32)
            gath[half(j, 1), c] = total.astype(bf16)
            return carry

        lax.fori_loop(0, depth // 512, tile, 0)

    def multiply(b, n_blocks):
        for k in range(n_blocks):
            remote(
                operand.at[block(0)], operands.at[block(b + k)], o_send.at[0], o_recv.at[b + k],
                section=1 - s,
            ).wait_recv()

        def tile(n, carry):
            part = lax.dot_general(
                operands[block(b, n_blocks), :], w[columns(n, 256), :],
                (((1,), (1,)), ((), ())), preferred_element_type=f32,
            )
            gath[block(b, n_blocks), columns(n, 256)] = part.astype(bf16)
            return carry

        lax.fori_loop(0, depth // 256, tile, 0)

    def second_product(i, code):
        zj = code % 8

        @pl.when(i == 0)
        def _():
            multiply(2 * zj + 1 - x, 1)

        @pl.when(i > 0)
        def _():
            multiply(2 * zj, 2)

        @pl.when(is_split(zj) & is_edge(z))
        def _():
            half_sums(zj // 3, lambda c: c.start())

        @pl.when(jnp.logical_not(is_edge(zj) & (zj == z)))
        def _():
            x_copy(zj, lambda c: c.start())

        @pl.when(i == 0)
        def _():
            multiply(2 * zj + x, 1)

    def hand(r, carry):
        hand_over(r).start()
        return carry

    lax.fori_loop(0, 4, hand, 0)

    def pass_on(i, carry):
        e = (i + z) % 2
        add_half(e)
        half_sums(e, lambda c: c.start())
        return carry

    def z_up(zj, h):
        return remote(
            x_in.at[half(zj, h)], z_in.at[half(zj, h)], zs_send.at[2 * zj + h],
            zs_recv.at[2 * zj + h], dp=(d + 2) % 8,
        )

    def z_down(zj, h):
        slot = jnp.where(zj == z - 1, 4, zj)
        return remote(
            x_in.at[half(zj, h)], z_in.at[half(slot, h)], zs_send.at[2 * zj + h],
            zs_recv.at[2 * slot + h], dp=(d + 6) % 8,
        )

    def arrived(slot, h):
        remote(
            x_in.at[half(0, h)], z_in.at[half(slot, h)], zs_send.at[h], zs_recv.at[2 * slot + h],
            dp=(d + 2) % 8,
        ).wait_recv()

    def gather_sums(i, code):
        zj = code % 8

        @pl.when((i == 2) & is_edge(z))
        def _():
            add_half(z // 3)
            x_copy(z, lambda c: c.start())

        x_copy(zj, lambda c: c.wait_recv())
        own = zj == z
        one = ((zj >= z) & (z > 0)) | ((zj < z) & (z < 3))
        two = own & (z < 3)

        def add(h, with_x, with_one, with_two):
            def tile(n, carry):
                c = columns(n, 512)
                total = gath[half(2 * zj + x, h), c].astype(f32)
                if with_x:
                    total = total + x_in[half(zj, h), c].astype(f32)
                if with_one:
                    total = total + z_in[half(zj, h), c].astype(f32)
                if with_two:
                    total = total + z_in[half(4, h), c].astype(f32)
                x_in[half(zj, h), c] = total.astype(bf16)
                return carry

            lax.fori_loop(0, depth // 512, tile, 0)

        for h in (0, 1):
            pl.when(one)(lambda: arrived(zj, h))
            pl.when(two)(lambda: arrived(4, h))
            for with_one in (False, True):
                for with_two in (False, True):
                    a = one if with_one else jnp.logical_not(one)
                    b = two if with_two else jnp.logical_not(two)
                    if h == 0:
                        pl.when(a & b)(functools.partial(add, 0, True, with_one, with_two))
                        continue
                    for with_x in (False, True):
                        if with_x or not with_two:
                            c = jnp.logical_not(is_split(zj)) if with_x else is_split(zj)
                            pl.when(a & b & c)(
                                functools.partial(add, 1, with_x, with_one, with_two)
                            )
            pl.when(zj > z)(lambda: z_up(zj, h).start())
            pl.when(zj < z)(lambda: z_down(zj, h).start())

    def sums_step(i, codes):
        product_code, sum_code = codes

        @pl.when(i < 4)
        def _():
            second_product(i, product_code)

        @pl.when((i == 2) & jnp.logical_not(is_edge(z)))
        def _():
            lax.fori_loop(0, 2, pass_on, 0)

        @pl.when(i >= 2)
        def _():
            gather_sums(i - 2, sum_code)

        return product_code // 8, jnp.where(i >= 2, sum_code // 8, sum_code)

    order = by_place(z, DESTINATIONS)
    lax.fori_loop(0, 6, sums_step, (order, order))
    store = pltpu.make_async_copy(x_in.at[block(z)], result, local_sem.at[2])
    store.start()

    def finish(r, carry):
        hand_over(r).wait()
        operand_near(r).wait_send()
        operand_far(r).wait_send()
        x_copy(r, lambda c: c.wait_send())

        @pl.when(r < 2)
        def _():
            half_sums(r, lambda c: c.wait_send())

        @pl.when(r > z)
        def _():
            for h in (0, 1):
                z_up(r, h).wait_send()

        @pl.when(r < z)
        def _():
            for h in (0, 1):
                z_down(r, h).wait_send()

        return carry

    lax.fori_loop(0, 4, finish, 0)
    store.wait()


def fused_local(section_weights, tensor_inputs, stream_inputs, ln_gain, ln_bias):
    weight = section_weights[0]
    incoming = tensor_inputs[0]
    saved = stream_inputs[0]
    depth, width = weight.shape
    bf16, f32 = jnp.bfloat16, jnp.float32
    sem = pltpu.SemaphoreType.DMA
    anywhere = pl.BlockSpec(memory_space=pl.ANY)
    vmem = pl.BlockSpec(memory_space=pltpu.VMEM)
    handed, result = pl.pallas_call(
        kernel,
        out_shape=(
            jax.ShapeDtypeStruct(saved.shape, bf16),
            jax.ShapeDtypeStruct(incoming.shape, bf16),
        ),
        in_specs=[anywhere, anywhere, vmem, vmem, vmem],
        out_specs=(anywhere, anywhere),
        scratch_shapes=[
            pltpu.VMEM((depth, width), bf16),
            pltpu.VMEM((1024, depth), bf16),
            pltpu.VMEM((512, width), f32),
            pltpu.VMEM((512, width), bf16),
            pltpu.VMEM((512, width), bf16),
            pltpu.VMEM((512, width), bf16),
            pltpu.VMEM((512, width), bf16),
            pltpu.VMEM((1024, width), bf16),
            pltpu.VMEM((512, depth), bf16),
            pltpu.VMEM((640, depth), bf16),
            pltpu.VMEM((128, depth), bf16),
            pltpu.VMEM((8, 32, 128), f32),
            pltpu.VMEM((8, 32, 128), f32),
            sem((3,)), sem((8,)), sem((4,)), sem((4,)), sem((4,)), sem((4,)), sem((4,)),
            sem((8,)), sem((8,)), sem((8,)), sem((8,)),
            sem((4,)), sem((4,)), sem((4,)), sem((4,)), sem((8,)),
            sem((4,)), sem((4,)), sem((8,)), sem((10,)),
            sem((2,)), sem((2,)), sem((2,)), sem((2,)),
        ],
        compiler_params=pltpu.CompilerParams(
            collective_id=0, has_side_effects=True, vmem_limit_bytes=64 * 1024 * 1024 - 65536
        ),
        cost_estimate=pl.CostEstimate(
            flops=4 * 1024 * depth * width, bytes_accessed=2 * depth * width, transcendentals=0
        ),
    )(weight, incoming, saved, ln_gain[None], ln_bias[None])
    return handed[None], result[None]


def solution(mesh):
    fused = dict(mesh.shape) == {"section": 2, "dp": 8, "mp": 2}
    in_specs = (
        P("section", "mp", "dp"),
        P("section", "dp", "mp"),
        P("section", "mp", "dp"),
        P("dp"),
        P("dp"),
    )
    out_specs = (P("section", "mp", "dp"), P("section", "dp", "mp"))
    body = fused_local if fused else local
    return jax.shard_map(body, mesh=mesh, in_specs=in_specs, out_specs=out_specs, check_vma=False)
```
